32 devices in a mesh: rep: 16 (over z, x, core), fsdp: 2 (over y).
Axes of the slice: x: 2, y: 2, z: 4, core: 2. Of those that a mesh axis runs over, the one named last changes fastest.
Arguments:
- tokens: bfloat16 [16, 1024, 4096], P('rep', 'fsdp'), may hold values from -6 to 6
- cotangent: bfloat16 [16, 1024, 512], P('rep', 'fsdp'), may hold values from -6 to 6
- doc_ids: int32 [16, 1024], P('rep', 'fsdp'), may hold values from 0 to 7, never falling along the last dimension, each value on 1 to 256 neighbouring positions
- pseudo_grads: float32 [16, 4096, 512], P('rep', 'fsdp'), may hold values from -2 to 2
- master: float32 [2, 2048, 512], P('fsdp', 'rep'), may hold values from -0.09375 to 0.09375
- momentum: float32 [2, 2048, 512], P('fsdp', 'rep'), may hold values from -0.15625 to 0.15625
Outputs:
- new_master: float32 [2, 2048, 512], P('fsdp', 'rep')
- new_momentum: float32 [2, 2048, 512], P('fsdp', 'rep')
- keys: bfloat16 [16, 1024, 512], P('rep', 'fsdp')
- weight_grad: bfloat16 [16, 4096, 512], P('rep', 'fsdp')
The draws below stay inside these ranges and needn't reach their ends.
Inputs may be any that keep to these rules, and one draw needn't show every extreme that they name: `doc_ids`: along each row the numbers never fall; each document has 1 to 256 tokens, and some document has exactly that many.
All inputs are finite; a program needn't handle non-finite values.
Results may differ from the reference program's by a relative error of at most 0.005.
Values may be sent and summed in bfloat16 or wider, within the bound.
No kernel may reach another device: no remote copies, remote signals or barrier semaphores. Data moves between devices by JAX's collectives and lax.ppermute only.
A program may use at most 64 MiB of HBM per device.

```python
import math
import jax
import jax.numpy as jnp
import numpy as np
from jax import lax

D = 4096
KV_COLS = 512
HEAD = 128
TOK_DEV = 512
REPLICAS = 16
SEQ = 1024
N_FSDP = 2


def strengthened(result, rng, source, target, blocks, factor):
    owner, partner = [(jnp.arange(result.shape[position]) // (result.shape[position] // blocks)).reshape([-1 if axis == position else 1 for axis in range(result.ndim)]) for position in (source, target)]
    chosen = jax.random.permutation(rng, blocks)[partner]
    strong = (owner == chosen) | (owner == (partner + blocks // 2) % blocks)
    return jnp.where(strong, factor * result, result)


def steps_of(rng, shape, pieces, smallest, largest):
    factor_of = 1.0
    for axis_at, parts in pieces:
        draws = jax.random.uniform(jax.random.fold_in(jax.random.fold_in(rng, 6), axis_at), (parts,), jnp.float32, smallest / len(pieces), largest / len(pieces))
        factor_of = factor_of * jnp.repeat(jnp.exp(draws), shape[axis_at] // parts).reshape((-1,) + (1,) * (len(shape) - 1 - axis_at))
    return factor_of


def length_profile(number_of, total, most, skew):
    portions = [(1 << 20) // math.isqrt(grade ** skew) + 1 for grade in range(2, number_of + 1)]
    rest, holding = total - most - (number_of - 1), [1] * (number_of - 1)
    while rest > 0:
        free = [i for i in range(number_of - 1) if holding[i] < most]
        whole, budget = sum([portions[i] for i in free]), rest
        for i in free:
            addition = min(most - holding[i], max(1, budget * portions[i] // whole), rest)
            holding[i] = holding[i] + addition
            rest = rest - addition
    return np.array([most] + holding)


def ragged_sizes(own_key, number_of, total, bound, slope):
    if number_of == 2:
        one = jax.random.randint(own_key, (), max(1, total - bound), min(bound, total - 1) + 1)
        return jnp.stack([one, total - one])
    lengths = jnp.asarray(length_profile(number_of, total, bound, slope), jnp.int32)
    pairs = (number_of - 1) // 2
    donor, sink = lengths[1:1 + 2 * pairs:2], lengths[2:2 + 2 * pairs:2]
    margin = jnp.minimum(donor - 1, bound - sink)
    passed = jax.random.randint(jax.random.fold_in(own_key, 1), (pairs,), 0, 1 << 20) % (margin + 1)
    lengths = lengths.at[1:1 + 2 * pairs:2].set(donor - passed).at[2:2 + 2 * pairs:2].set(sink + passed)
    return lengths[jax.random.permutation(jax.random.fold_in(own_key, 2), number_of)]


def centred(rng, extent, width, bound, split=(), kind=jnp.bfloat16):
    result = jax.random.normal(rng, extent, jnp.float32) * width
    if len(split) > 0:
        result = steps_of(rng, extent, split, -0.22, 0.18) * result
    return jnp.clip(result, min=-bound, max=bound).astype(kind)


def heavy_noise(key, extent, width, reach, cuts, heavy, held_as=jnp.bfloat16):
    values = width * jax.random.normal(key, extent, jnp.float32)
    if cuts:
        values = values * steps_of(key, extent, cuts, -0.22, 0.18)
    return jnp.clip(strengthened(values, jax.random.fold_in(key, 3), *heavy), -reach, reach).astype(held_as)


def setup_inputs(seed: int = 0) -> dict:
    key_list = jax.random.split(jax.random.key(seed), 7)
    return {
        "tokens": centred(key_list[0], (REPLICAS, SEQ, D), 1.0, 6.0, ((0, 16), (1, 2))),
        "cotangent": centred(key_list[1], (REPLICAS, SEQ, KV_COLS), 1.0, 6.0, ((0, 16), (1, 2))),
        "doc_ids": jax.vmap(lambda own: jnp.searchsorted(jnp.cumsum(ragged_sizes(own, 4 * N_FSDP, SEQ, TOK_DEV // 2, 0)), jnp.arange(SEQ), side="right"))(jax.random.split(key_list[2], REPLICAS)).reshape((REPLICAS, SEQ)).astype(jnp.int32),
        "pseudo_grads": heavy_noise(key_list[3], (REPLICAS, D, KV_COLS), 0.1, 2.0, ((0, 16), (1, 2)), (0, 1, 16, 2.0), jnp.float32),
        "master": centred(key_list[4], (N_FSDP, D // N_FSDP, KV_COLS), D ** -0.5, 0.09375, ((0, 2), (1, 16)), jnp.float32),
        "momentum": centred(key_list[5], (N_FSDP, D // N_FSDP, KV_COLS), 0.01, 0.15625, ((0, 2), (1, 16)), jnp.float32),
    }


def rotate(values, positions, sign):
    count = values.shape[0]
    heads = values.reshape(count, -1, HEAD)
    freqs = 500000.0 ** (-jnp.arange(HEAD // 2, dtype=jnp.float32) / (HEAD // 2))
    angles = positions.astype(jnp.float32)[:, None] * freqs[None, :]
    cosine = jnp.cos(angles)[:, None, :]
    sine = sign * jnp.sin(angles)[:, None, :]
    first = heads[..., : HEAD // 2]
    second = heads[..., HEAD // 2:]
    turned = jnp.concatenate([first * cosine - second * sine, second * cosine + first * sine], axis=-1)
    return turned.reshape(count, -1)


def doc_positions(documents):
    count = documents.shape[0]
    places = jnp.arange(count, dtype=jnp.int32)
    changed = jnp.concatenate([jnp.ones((1,), dtype=bool), documents[1:] != documents[:-1]])
    starts = lax.cummax(jnp.where(changed, places, 0), axis=0)
    return places - starts


def reference(tokens, cotangent, doc_ids, pseudo_grads, master, momentum):
    outer_delta = jnp.sum(pseudo_grads, axis=0) / REPLICAS
    flat_master = master.reshape(D, KV_COLS)
    flat_momentum = momentum.reshape(D, KV_COLS)
    new_momentum = 0.9 * flat_momentum + outer_delta
    new_master = flat_master - 0.7 * (outer_delta + 0.9 * new_momentum)
    weights = new_master.astype(jnp.bfloat16)

    def replica(items):
        features, upstream, documents = items
        positions = doc_positions(documents)
        projected = jnp.dot(features, weights, preferred_element_type=jnp.float32)
        keys_row = rotate(projected, positions, 1.0).astype(jnp.bfloat16)
        rotated = rotate(upstream.astype(jnp.float32), positions, -1.0).astype(jnp.bfloat16)
        grads = jnp.dot(features.T, rotated, preferred_element_type=jnp.float32).astype(jnp.bfloat16)
        return keys_row, grads

    keys, weight_grad = lax.map(replica, (tokens, cotangent, doc_ids))
    return (new_master.reshape(master.shape), new_momentum.reshape(master.shape), keys, weight_grad)
```

```python
import math

import jax
import jax.numpy as jnp
from jax import lax
from jax.sharding import PartitionSpec as P

HEAD = 128
LINK = jnp.bfloat16


def factors_of(count):
    parts = []
    for size in (2, 2, 4):
        if count % size == 0 and count > 1:
            parts.append(size)
            count //= size
    if count > 1:
        parts.append(count)
    return parts


def shift_pairs(count, stride, size, step):
    pairs = []
    for source in range(count):
        part = source // stride % size
        pairs.append((source, source + ((part + step) % size - part) * stride))
    return pairs


def picked(value, index, axis):
    return lax.dynamic_index_in_dim(value, index, axis, keepdims=False)


def tables(positions):
    freqs = 500000.0 ** (-jnp.arange(HEAD // 2, dtype=jnp.float32) / (HEAD // 2))
    angles = positions.astype(jnp.float32)[:, None] * freqs[None, :]
    return jnp.cos(angles)[:, None, :], jnp.sin(angles)[:, None, :]


def rotate(values, cosine, sine):
    count = values.shape[0]
    heads = values.reshape(count, -1, HEAD)
    first = heads[..., : HEAD // 2]
    second = heads[..., HEAD // 2 :]
    turned = jnp.concatenate(
        [first * cosine - second * sine, second * cosine + first * sine], axis=-1
    )
    return turned.reshape(count, -1)


def local(tokens, cotangent, doc_ids, pseudo_grads, master, momentum):
    reps = lax.axis_size("rep")
    pair = lax.axis_size("fsdp")
    rep = lax.axis_index("rep")
    side = lax.axis_index("fsdp")
    parts = factors_of(reps)
    band, columns = master.shape[1:]
    features = tokens[0]
    count, width = features.shape
    depth = width // pair

    strides = [math.prod(parts[:i]) for i in range(len(parts))]
    places = [rep // stride % size for stride, size in zip(strides, parts)]
    terms = [pseudo_grads[0].reshape(tuple(reversed(parts)) + (band, columns))]
    for level, (stride, size, place) in enumerate(zip(strides, parts, places)):
        axis = len(parts) - 1 - level
        kind = jnp.float32 if level == 0 else LINK
        received = []
        for step in range(1, size):
            chosen = sum(picked(t, (place + step) % size, axis).astype(jnp.float32) for t in terms)
            received.append(
                lax.ppermute(chosen.astype(kind), "rep", shift_pairs(reps, stride, size, step))
            )
        terms = [picked(t, place, axis) for t in terms] + received

    documents = doc_ids[0]
    halves = {0: (picked(features.reshape(count, pair, depth), side, 1), cotangent[0], documents)}
    for step in range(1, pair):
        pairs = shift_pairs(pair, 1, pair, step)
        wanted = picked(features.reshape(count, pair, depth), (side + step) % pair, 1)
        halves[(pair - step) % pair] = (
            lax.ppermute(wanted, "fsdp", pairs),
            lax.ppermute(cotangent[0], "fsdp", pairs),
            lax.ppermute(documents, "fsdp", pairs),
        )

    outer_delta = sum(t.astype(jnp.float32) for t in terms) / reps
    new_momentum = 0.9 * momentum[0] + outer_delta
    new_master = master[0] - 0.7 * (outer_delta + 0.9 * new_momentum)

    held = new_master.astype(LINK)[None]
    for stride, size, place in reversed(list(zip(strides, parts, places))):
        pieces = [held] + [
            lax.ppermute(held, "rep", shift_pairs(reps, stride, size, size - step))
            for step in range(1, size)
        ]
        joined = jnp.stack(pieces, axis=1)
        rolled = jnp.concatenate([joined, joined[:, : size - 1]], axis=1)
        held = lax.dynamic_slice_in_dim(rolled, (size - place) % size, size, axis=1)
        held = held.reshape((-1, band, columns))
    weights = held.reshape(depth, columns)

    all_documents = jnp.concatenate([half[2] for half in halves.values()])
    grads = jnp.zeros((depth, columns), jnp.float32)
    turns = {}
    for step, (part, upstream, docs) in halves.items():
        at = (side + step) % pair * count + jnp.arange(count, dtype=jnp.int32)
        starts = jnp.sum((all_documents[None, :] < docs[:, None]).astype(jnp.int32), axis=1)
        turns[step] = tables(at - starts)
        cosine, sine = turns[step]
        rotated = rotate(upstream.astype(jnp.float32), cosine, -sine).astype(jnp.bfloat16)
        grads = grads + lax.dot_general(
            part, rotated, (((0,), (0,)), ((), ())), preferred_element_type=jnp.float32
        )

    projected = jnp.float32(0)
    for step in range(pair - 1, -1, -1):
        product = jnp.dot(halves[step][0], weights, preferred_element_type=jnp.float32)
        if step:
            product = lax.ppermute(
                product.astype(LINK), "fsdp", shift_pairs(pair, 1, pair, step)
            ).astype(jnp.float32)
        projected = projected + product
    keys = rotate(projected, *turns[0]).astype(jnp.bfloat16)
    return (
        new_master[None],
        new_momentum[None],
        keys[None],
        grads.astype(jnp.bfloat16)[None],
    )


def solution(mesh):
    return jax.shard_map(
        local,
        mesh=mesh,
        in_specs=(
            P("rep", "fsdp", None),
            P("rep", "fsdp", None),
            P("rep", "fsdp"),
            P("rep", "fsdp", None),
            P("fsdp", "rep", None),
            P("fsdp", "rep", None),
        ),
        out_specs=(
            P("fsdp", "rep", None),
            P("fsdp", "rep", None),
            P("rep", "fsdp", None),
            P("rep", "fsdp", None),
        ),
        check_vma=False,
    )
```

```python
import functools
import math

import jax
import jax.numpy as jnp
from jax import lax
from jax.experimental import pallas as pl
from jax.experimental.pallas import tpu as pltpu
from jax.sharding import PartitionSpec as P

HEAD = 128
LINK = jnp.bfloat16


def factors_of(count):
    parts = []
    for size in (2, 2, 4):
        size = math.gcd(size, count)
        parts.append(size)
        count //= size
    return parts + [count]


def shift_pairs(count, stride, size, step):
    pairs = []
    for source in range(count):
        part = source // stride % size
        pairs.append((source, source + ((part + step) % size - part) * stride))
    return pairs


def picked(value, index, axis):
    return lax.dynamic_index_in_dim(value, index, axis, keepdims=False)


def total(terms):
    return sum(t.astype(jnp.float32) for t in terms)


def tables(positions):
    freqs = 500000.0 ** (-jnp.arange(HEAD // 2, dtype=jnp.float32) / (HEAD // 2))
    angles = positions.astype(jnp.float32)[:, None] * freqs[None, :]
    cosine, sine = jnp.cos(angles), jnp.sin(angles)
    return jnp.concatenate([cosine, cosine], axis=1), jnp.concatenate([-sine, sine], axis=1)


def turned(block, cosine, sine):
    return block * cosine + pltpu.roll(block, HEAD // 2, 1) * sine


def turn_kernel(sign, value_ref, cosine_ref, sine_ref, out_ref):
    cosine, sine = cosine_ref[...], sine_ref[...] * sign
    for head in range(value_ref.shape[1] // HEAD):
        at = pl.ds(head * HEAD, HEAD)
        block = value_ref[:, at].astype(jnp.float32)
        out_ref[:, at] = turned(block, cosine, sine).astype(out_ref.dtype)


def turn(value, cosine, sine, sign):
    return pl.pallas_call(
        functools.partial(turn_kernel, sign),
        out_shape=jax.ShapeDtypeStruct(value.shape, jnp.bfloat16),
        name="turn",
    )(value, cosine, sine)


def finish_kernel(own_ref, other_ref, cosine_ref, sine_ref, out_ref):
    cosine, sine = cosine_ref[...], sine_ref[...]
    for head in range(own_ref.shape[1] // HEAD):
        at = pl.ds(head * HEAD, HEAD)
        block = own_ref[:, at] + other_ref[:, at].astype(jnp.float32)
        out_ref[:, at] = turned(block, cosine, sine).astype(out_ref.dtype)


def finish(own, other, cosine, sine):
    return pl.pallas_call(
        finish_kernel,
        out_shape=jax.ShapeDtypeStruct(own.shape, jnp.bfloat16),
        name="finish",
    )(own, other, cosine, sine)


def project_kernel(count, place_ref, part_ref, *refs):
    bands, (out_ref, weights_ref) = refs[:count], refs[count:]
    at = 0
    for ref in bands:
        for i in range(ref.shape[0]):
            rows = ref.shape[1]
            start = pl.multiple_of(place_ref[at] * rows, rows)
            weights_ref[pl.ds(start, rows), :] = ref[i]
            at += 1
    out_ref[...] = jnp.dot(
        part_ref[...], weights_ref[...], preferred_element_type=jnp.float32
    ).astype(out_ref.dtype)


def project(places, part, bands):
    rows = sum(b.shape[0] * b.shape[1] for b in bands)
    columns = bands[0].shape[2]
    vmem = pl.BlockSpec(memory_space=pltpu.VMEM)
    return pl.pallas_call(
        functools.partial(project_kernel, len(bands)),
        in_specs=[pl.BlockSpec(memory_space=pltpu.SMEM)] + [vmem] * (1 + len(bands)),
        out_specs=[vmem, vmem],
        out_shape=[
            jax.ShapeDtypeStruct((part.shape[0], columns), LINK),
            jax.ShapeDtypeStruct((rows, columns), LINK),
        ],
        compiler_params=pltpu.CompilerParams(vmem_limit_bytes=40 * 1024 * 1024),
        name="project",
    )(places, part, *bands)


def local(tokens, cotangent, doc_ids, pseudo_grads, master, momentum):
    reps = lax.axis_size("rep")
    pair = lax.axis_size("fsdp")
    rep = lax.axis_index("rep")
    side = lax.axis_index("fsdp")
    parts = factors_of(reps)
    strides = [math.prod(parts[:i]) for i in range(len(parts))]
    place = [rep // stride % size for stride, size in zip(strides, parts)]
    band, columns = master.shape[1:]
    features = tokens[0]
    count, width = features.shape
    depth = width // pair

    def moved(value, level, step):
        pairs = shift_pairs(reps, strides[level], parts[level], step)
        return lax.ppermute(value, "rep", pairs)

    def across(value, step):
        return lax.ppermute(value, "fsdp", shift_pairs(pair, 1, pair, step))

    def half_of(step):
        return lax.dynamic_slice_in_dim(features, (side + step) % pair * depth, depth, 1)

    fast, middle, slow, rest = parts
    mine = pseudo_grads[0].reshape(rest, slow, middle, fast, band, columns)
    sent = [picked(mine, (place[0] + k) % fast, 3).astype(LINK) for k in range(1, fast)]
    documents = doc_ids[0]
    wanted = [half_of(step) for step in range(1, pair)]
    sent, wanted = lax.optimization_barrier((sent, wanted))
    terms = [moved(t, 0, k + 1) for k, t in enumerate(sent)]

    halves = {0: (half_of(0), cotangent[0], documents)}
    for step in range(1, pair):
        halves[(pair - step) % pair] = (
            across(wanted[step - 1], step),
            across(cotangent[0], step),
            across(documents, step),
        )

    terms = [picked(mine, place[0], 3)] + terms
    received = []
    own = None
    for k in list(range(1, slow)) + [0]:
        slices = [picked(t, (place[2] + k) % slow, 1) for t in terms]
        piece = [picked(t, place[1], 1) for t in slices]
        for step in range(1, middle):
            chosen = total([picked(t, (place[1] + step) % middle, 1) for t in slices])
            piece.append(moved(chosen.astype(LINK), 1, step))
        if k:
            received.append(moved(total(piece).astype(LINK), 2, k))
        else:
            own = piece
    terms = own + received
    here = [picked(t, place[3], 0) for t in terms]
    for step in range(1, rest):
        chosen = total([picked(t, (place[3] + step) % rest, 0) for t in terms])
        here.append(moved(chosen.astype(LINK), 3, step))

    outer_delta = total(here) / reps
    new_momentum = 0.9 * momentum[0] + outer_delta
    new_master = master[0] - 0.7 * (outer_delta + 0.9 * new_momentum)

    held = new_master.astype(LINK)[None]
    pieces = [(held, [0])] + [(moved(held, 3, rest - k), [k]) for k in range(1, rest)]
    held = jnp.concatenate([piece for piece, _ in pieces])
    outer = [(place[3] + k) % rest * strides[3] for k in range(rest)]
    first = [(held if k == 0 else moved(held, 2, slow - k), k) for k in range(slow)]
    bands, places = [], []
    for shift in range(middle):
        group = [piece if shift == 0 else moved(piece, 1, middle - shift) for piece, _ in first]
        spots = [
            o + (place[2] + k) % slow * strides[2] + (place[1] + shift) % middle * strides[1]
            for _, k in first
            for o in outer
        ]
        bands += group
        places += [spot + place[0] for spot in spots]
        joined = jnp.concatenate(group)
        for step in range(1, fast):
            bands.append(moved(joined, 0, fast - step))
            places += [spot + (place[0] + step) % fast for spot in spots]
    places = jnp.stack(places)

    grads = jnp.zeros((depth, columns), jnp.float32)
    turns = {}
    for step, (part, upstream, docs) in halves.items():
        at = (side + step) % pair * count + jnp.arange(count, dtype=jnp.int32)
        for _, _, others in halves.values():
            at = at - jnp.sum((others[None, :] < docs[:, None]).astype(jnp.int32), axis=1)
        turns[step] = tables(at)
        rotated = turn(upstream, *turns[step], -1.0)
        grads = grads + lax.dot_general(
            part, rotated, (((0,), (0,)), ((), ())), preferred_element_type=jnp.float32
        )

    weights = None
    other = 0
    for step in range(1, pair):
        if weights is None:
            product, weights = project(places, halves[step][0], bands)
        else:
            product = jnp.dot(halves[step][0], weights, preferred_element_type=jnp.float32)
        other = other + across(product.astype(LINK), step)
    product = jnp.dot(halves[0][0], weights, preferred_element_type=jnp.float32)
    keys = finish(product, other, *turns[0])
    return (
        new_master[None],
        new_momentum[None],
        keys[None],
        grads.astype(jnp.bfloat16)[None],
    )


def solution(mesh):
    return jax.shard_map(
        local,
        mesh=mesh,
        in_specs=(
            P("rep", "fsdp", None),
            P("rep", "fsdp", None),
            P("rep", "fsdp"),
            P("rep", "fsdp", None),
            P("fsdp", "rep", None),
            P("fsdp", "rep", None),
        ),
        out_specs=(
            P("fsdp", "rep", None),
            P("fsdp", "rep", None),
            P("rep", "fsdp", None),
            P("rep", "fsdp", None),
        ),
        check_vma=False,
    )
```

```python
import functools
import math

import jax
import jax.numpy as jnp
from jax import lax
from jax.experimental import pallas as pl
from jax.experimental.pallas import tpu as pltpu
from jax.sharding import PartitionSpec as P

HEAD = 128
LINK = jnp.bfloat16


def factors_of(count):
    parts = []
    for size in (2, 2, 4):
        size = math.gcd(size, count)
        parts.append(size)
        count //= size
    return parts + [count]


def shift_pairs(count, stride, size, step):
    pairs = []
    for source in range(count):
        part = source // stride % size
        pairs.append((source, source + ((part + step) % size - part) * stride))
    return pairs


def picked(value, index, axis):
    return lax.dynamic_index_in_dim(value, index, axis, keepdims=False)


def total(terms):
    return sum(t.astype(jnp.float32) for t in terms)


def tables(positions):
    freqs = 500000.0 ** (-(jnp.arange(HEAD) % (HEAD // 2)).astype(jnp.float32) / (HEAD // 2))
    angles = positions.astype(jnp.float32)[:, None] * freqs[None, :]
    sign = jnp.where(jnp.arange(HEAD) < HEAD // 2, -1.0, 1.0)
    return jnp.cos(angles), jnp.sin(angles) * sign[None, :]


def after(value, *before):
    return lax.optimization_barrier((value, before))[0]


VMEM = pl.BlockSpec(memory_space=pltpu.VMEM)
PLAIN = pl.BlockSpec(memory_space=pltpu.HBM)


CHEAP = pl.CostEstimate(flops=0, bytes_accessed=0, transcendentals=0)
PARAMS = pltpu.CompilerParams(vmem_limit_bytes=24 * 1024 * 1024)


def turned(block, cosine, sine):
    return block * cosine + pltpu.roll(block, HEAD // 2, 1) * sine


def pack_kernel(
    parts, place_ref, features_ref, documents_ref, sums_ref, out_ref, core_ref, held_ref, wide_ref, half_ref, sems
):
    count, depth = features_ref.shape[0], out_ref.shape[1]
    fast, band = sums_ref.shape[1], sums_ref.shape[2]
    blocks = sums_ref.shape[0]
    at = pl.ds(pl.multiple_of(place_ref[0] * depth, depth), depth)
    ins, outs, wide, half = [], [], [], []
    for i in range(blocks):
        wide.append(
            pltpu.make_async_copy(sums_ref.at[i, place_ref[1]], wide_ref.at[i], sems.at[2, i])
        )
        half.append(pltpu.make_async_copy(half_ref.at[i], core_ref.at[i], sems.at[3, i]))
        wide[-1].start()
    for i in range(parts):
        rows = pl.ds(i * (count // parts), count // parts)
        ins.append(
            pltpu.make_async_copy(features_ref.at[rows, at], held_ref.at[rows, :], sems.at[0, i])
        )
        outs.append(pltpu.make_async_copy(held_ref.at[rows, :], out_ref.at[rows, :], sems.at[1, i]))
        ins[-1].start()
    rows = pl.ds(count, out_ref.shape[0] - count)
    held_ref[rows, :] = jnp.zeros((rows.size, depth), out_ref.dtype)
    held_ref[rows, pl.ds(0, count)] = jnp.broadcast_to(
        documents_ref[...].astype(jnp.float32).astype(out_ref.dtype), (rows.size, count)
    )
    outs.append(pltpu.make_async_copy(held_ref.at[rows, :], out_ref.at[rows, :], sems.at[1, parts]))
    outs[-1].start()
    for i in range(blocks):
        wide[i].wait()
        half_ref[i] = wide_ref[i].astype(half_ref.dtype)
        half[i].start()
    for i in range(parts):
        ins[i].wait()
        outs[i].start()
    for copy in half + outs:
        copy.wait()


def pack(place, features, documents, sums, depth, parts=8, note=16):
    shape = (features.shape[0] + note, depth)
    blocks, _, band, columns = sums.shape
    plain = pl.BlockSpec(memory_space=pltpu.HBM)
    return pl.pallas_call(
        functools.partial(pack_kernel, parts),
        in_specs=[pl.BlockSpec(memory_space=pltpu.SMEM), plain, VMEM, plain],
        out_specs=[plain, plain],
        out_shape=[
            jax.ShapeDtypeStruct(shape, features.dtype),
            jax.ShapeDtypeStruct((blocks, band, columns), LINK),
        ],
        scratch_shapes=[
            pltpu.VMEM(shape, features.dtype),
            pltpu.VMEM((blocks, band, columns), sums.dtype),
            pltpu.VMEM((blocks, band, columns), LINK),
            pltpu.SemaphoreType.DMA((4, max(parts + 1, blocks))),
        ],
        compiler_params=pltpu.CompilerParams(vmem_limit_bytes=60 * 1024 * 1024),
        cost_estimate=CHEAP,
        name="pack",
    )(place, features, documents, sums)


def turn_into(out_ref, start, value, cosine, sine):
    for head in range(value.shape[1] // HEAD):
        block = value[:, head * HEAD : (head + 1) * HEAD].astype(jnp.float32)
        block = turned(block, cosine, -sine).astype(out_ref.dtype)
        out_ref[pl.ds(start, value.shape[0]), pl.ds(head * HEAD, HEAD)] = block


def gradient_kernel(side_ref, own_ref, value_ref, cosine_ref, sine_ref, *refs):
    out_ref, rotated_ref = refs[-2:]
    others = [refs[i : i + 4] for i in range(0, len(refs) - 2, 4)]
    count, columns = value_ref.shape

    @pl.when(pl.program_id(0) == 0)
    def _():
        turn_into(rotated_ref, 0, value_ref[...], cosine_ref[...], sine_ref[...])
        for i, (_, value, cosine, sine) in enumerate(others):
            turn_into(rotated_ref, (i + 1) * count, value[...], cosine[...], sine[...])

    tiles = [own_ref[...]] + [ref[...] for other in others for ref in other[:1]]
    out_ref[...] = lax.dot_general(
        jnp.concatenate(tiles, axis=0),
        rotated_ref[...],
        (((0,), (0,)), ((), ())),
        preferred_element_type=jnp.float32,
    ).astype(out_ref.dtype)


def gradient(side, features, value, tables_, others, depth, tile=256):
    count, columns = value.shape
    tiles = depth // tile
    table = pl.BlockSpec((count, HEAD), lambda i, side: (0, 0))
    specs, operands = [], []
    for other in others:
        specs += [
            pl.BlockSpec((count, tile), lambda i, side: (0, i)),
            pl.BlockSpec((count, columns), lambda i, side: (0, 0)),
            table,
            table,
        ]
        operands += other
    return pl.pallas_call(
        gradient_kernel,
        grid_spec=pltpu.PrefetchScalarGridSpec(
            num_scalar_prefetch=1,
            grid=(tiles,),
            in_specs=[
                pl.BlockSpec((count, tile), lambda i, side: (0, side[0] * tiles + i)),
                pl.BlockSpec((count, columns), lambda i, side: (0, 0)),
                table,
                table,
            ]
            + specs,
            out_specs=pl.BlockSpec((tile, columns), lambda i, side: (i, 0)),
            scratch_shapes=[pltpu.VMEM(((len(others) + 1) * count, columns), jnp.bfloat16)],
        ),
        out_shape=jax.ShapeDtypeStruct((depth, columns), jnp.bfloat16),
        compiler_params=PARAMS,
        cost_estimate=CHEAP,
        name="gradient",
    )(side, features, value, *tables_, *operands)


def rotated_into(out_ref, product, cosine_ref, sine_ref):
    cosine, sine = cosine_ref[...], sine_ref[...]
    for head in range(product.shape[1] // HEAD):
        block = product[:, head * HEAD : (head + 1) * HEAD]
        out_ref[:, pl.ds(head * HEAD, HEAD)] = turned(block, cosine, sine).astype(out_ref.dtype)


def product_kernel(side_ref, part_ref, weights_ref, cosine_ref, sine_ref, out_ref, sum_ref):
    at = pl.program_id(0)
    tile = jnp.dot(part_ref[...], weights_ref[...], preferred_element_type=jnp.float32)

    @pl.when(at == 0)
    def _():
        sum_ref[...] = tile

    @pl.when(at > 0)
    def _():
        sum_ref[...] += tile

    @pl.when(at == pl.num_programs(0) - 1)
    def _():
        rotated_into(out_ref, sum_ref[...], cosine_ref, sine_ref)


def product(side, part, weights, cosine, sine, kind, tile=512):
    depth, columns = weights.shape
    tiles, count = depth // tile, cosine.shape[0]
    table = pl.BlockSpec((count, HEAD), lambda i, side: (0, 0))
    return pl.pallas_call(
        product_kernel,
        grid_spec=pltpu.PrefetchScalarGridSpec(
            num_scalar_prefetch=1,
            grid=(tiles,),
            in_specs=[
                pl.BlockSpec((count, tile), lambda i, side: (0, side[0] * tiles + i)),
                pl.BlockSpec((tile, columns), lambda i, side: (i, 0)),
                table,
                table,
            ],
            out_specs=pl.BlockSpec((count, columns), lambda i, side: (0, 0)),
            scratch_shapes=[pltpu.VMEM((count, columns), jnp.float32)],
        ),
        out_shape=jax.ShapeDtypeStruct((count, columns), kind),
        compiler_params=PARAMS,
        cost_estimate=CHEAP,
        name="product",
    )(side, part, weights, cosine, sine)


def project_kernel(count, place_ref, part_ref, cosine_ref, sine_ref, *refs):
    bands, (out_ref, weights_ref, held_ref, sems, part_sems) = refs[:count], refs[count:]
    copies = []
    for ref in bands:
        for i in range(ref.shape[0]):
            rows, at = ref.shape[1], len(copies)
            start = pl.multiple_of(place_ref[at] * rows, rows)
            to = weights_ref.at[pl.ds(start, rows), :]
            copies.append(pltpu.make_async_copy(ref.at[i], to, sems.at[at]))
            copies[-1].start()
    tiles = part_sems.shape[0]
    tile = part_ref.shape[1] // tiles
    parts = []
    rows = pl.ds(0, held_ref.shape[0])
    for i in range(tiles):
        at = pl.ds(i * tile, tile)
        parts.append(
            pltpu.make_async_copy(part_ref.at[rows, at], held_ref.at[:, at], part_sems.at[i])
        )
        parts[-1].start()
    for copy in copies:
        copy.wait()
    product = jnp.zeros(out_ref.shape, jnp.float32)
    for i in range(tiles):
        parts[i].wait()
        at = pl.ds(i * tile, tile)
        product += jnp.dot(
            held_ref[:, at], weights_ref[at, :], preferred_element_type=jnp.float32
        )
    rotated_into(out_ref, product, cosine_ref, sine_ref)


def project(places, part, cosine, sine, bands, tiles=4):
    rows = sum(b.shape[0] * b.shape[1] for b in bands)
    columns = bands[0].shape[2]
    return pl.pallas_call(
        functools.partial(project_kernel, len(bands)),
        in_specs=[pl.BlockSpec(memory_space=pltpu.SMEM), PLAIN, VMEM, VMEM] + [PLAIN] * len(bands),
        out_specs=[VMEM, VMEM],
        out_shape=[
            jax.ShapeDtypeStruct((cosine.shape[0], columns), LINK),
            jax.ShapeDtypeStruct((rows, columns), LINK),
        ],
        scratch_shapes=[
            pltpu.VMEM((cosine.shape[0], rows), part.dtype),
            pltpu.SemaphoreType.DMA((places.shape[0],)),
            pltpu.SemaphoreType.DMA((tiles,)),
        ],
        compiler_params=PARAMS,
        cost_estimate=CHEAP,
        name="project",
    )(places, part, cosine, sine, *bands)


def local(tokens, cotangent, doc_ids, pseudo_grads, master, momentum):
    reps = lax.axis_size("rep")
    pair = lax.axis_size("fsdp")
    rep = lax.axis_index("rep")
    side = lax.axis_index("fsdp")
    parts = factors_of(reps)
    strides = [math.prod(parts[:i]) for i in range(len(parts))]
    place = [rep // stride % size for stride, size in zip(strides, parts)]
    band, columns = master.shape[1:]
    features = tokens[0]
    count, width = features.shape
    depth = width // pair

    def moved(value, level, step):
        pairs = shift_pairs(reps, strides[level], parts[level], step)
        return lax.ppermute(value, "rep", pairs)

    def across(value, step):
        return lax.ppermute(value, "fsdp", shift_pairs(pair, 1, pair, step))

    def half_of(step):
        return lax.dynamic_slice_in_dim(features, (side + step) % pair * depth, depth, 1)

    fast, middle, slow, rest = parts
    mine = pseudo_grads[0].reshape(rest, slow, middle, fast, band, columns)
    order = sorted(range(slow), key=lambda k: -min(k, slow - k))

    documents = doc_ids[0]
    which = side.astype(jnp.int32).reshape(1)
    bands = pseudo_grads[0].reshape(-1, fast, band, columns)
    sent, out = [], []
    for step in range(1, max(pair, fast)):
        goes = jnp.stack([(side + step) % pair, (place[0] + step) % fast]).astype(jnp.int32)
        one, two = pack(goes, features, doc_ids, bands, depth)
        sent += [one] if step < pair else []
        out += [two.reshape(rest, slow, middle, band, columns)] if step < fast else []
    parted = [None] + [across(t, i + 1) for i, t in enumerate(sent)][::-1]

    cores = [moved(t, 0, i + 1) for i, t in enumerate(out)]

    def piece(k, step):
        terms = [picked(mine, place[0], 3)] + cores
        terms = [picked(t, (place[2] + k) % slow, 1) for t in terms]
        return [picked(t, (place[1] + step) % middle, 1) for t in terms]

    out = {k: [total(piece(k, i)).astype(LINK) for i in range(1, middle)] for k in order}
    sums = {k: [moved(t, 1, i + 1) for i, t in enumerate(out[k])] for k in order}
    last = out
    received = []
    for k in order:
        if k:
            out = total(piece(k, 0) + after(sums[k], last)).astype(LINK)
            last = out
            received.append(moved(out, 2, k))
        else:
            received = piece(k, 0) + sums[k] + received
    here = [picked(t, place[3], 0) for t in received]
    for step in range(1, rest):
        chosen = total([picked(t, (place[3] + step) % rest, 0) for t in received])
        here.append(moved(chosen.astype(LINK), 3, step))
    upstream = after(cotangent[0], last)
    upstream = [None] + [across(upstream, pair - step) for step in range(1, pair)]

    def updated(delta):
        new_momentum = 0.9 * momentum[0] + delta
        return master[0] - 0.7 * (delta + 0.9 * new_momentum), new_momentum

    outer_delta = total(here) / reps

    held = updated(outer_delta)[0].astype(LINK)[None]
    held = jnp.concatenate([held] + [moved(held, 3, rest - k) for k in range(1, rest)])
    outer = [(place[3] + k) % rest * strides[3] for k in range(rest)]
    order = sorted(range(slow), key=lambda k: min(k, slow - k))
    slows = {k: held if k == 0 else moved(held, 2, slow - k) for k in order}
    crossed = {
        (k, shift): moved(slows[k], 1, middle - shift) for shift in range(1, middle) for k in order
    }
    near = [key for key in crossed if key[0] != order[-1]]
    last = [key for key in crossed if key[0] == order[-1]]
    groups = [[(k, 0) for k in order], near + last]
    crossed.update({(k, 0): slows[k] for k in order})
    bands, places = [], []
    for keys in groups:
        if not keys:
            continue
        group = [crossed[key] for key in keys]
        base = [
            o + (place[2] + k) % slow * strides[2] + (place[1] + shift) % middle * strides[1]
            for k, shift in keys
            for o in outer
        ]
        joined = group[0] if len(group) == 1 else jnp.concatenate(group)
        bands += group
        places += [spot + place[0] for spot in base]
        for step in range(1, fast):
            bands.append(moved(joined, 0, fast - step))
            places += [spot + (place[0] + step) % fast for spot in base]
    places = jnp.stack(places)

    early = [documents] + [
        part[count, :count].astype(jnp.int32) for part in parted[1:]
    ]
    turns = []
    for step, docs in enumerate(early):
        at = (side + step) % pair * count + jnp.arange(count, dtype=jnp.int32)
        for others in early:
            at = at - jnp.sum((others[None, :] < docs[:, None]).astype(jnp.int32), axis=1)
        turns.append(tables(at))

    weights = None
    other = []
    none = jnp.zeros((1,), jnp.int32)
    for step in range(1, pair):
        if weights is None:
            out, weights = project(places, parted[step], *turns[step], bands)
        else:
            out = product(none, parted[step], weights, *turns[step], LINK)
        other.append(across(out, pair - step))
    features = after(features, weights)
    grads = gradient(
        which,
        features,
        cotangent[0],
        turns[0],
        [(parted[step], upstream[step], *turns[step]) for step in range(1, pair)],
        depth,
    )
    keys = total([product(which, features, weights, *turns[0], jnp.float32)] + other)
    keys = keys.astype(jnp.bfloat16)
    new_master, new_momentum = updated(after(outer_delta, weights))
    return (
        new_master[None],
        new_momentum[None],
        keys[None],
        grads[None],
    )


def solution(mesh):
    return jax.shard_map(
        local,
        mesh=mesh,
        in_specs=(
            P("rep", "fsdp", None),
            P("rep", "fsdp", None),
            P("rep", "fsdp"),
            P("rep", "fsdp", None),
            P("fsdp", "rep", None),
            P("fsdp", "rep", None),
        ),
        out_specs=(
            P("fsdp", "rep", None),
            P("fsdp", "rep", None),
            P("rep", "fsdp", None),
            P("rep", "fsdp", None),
        ),
        check_vma=False,
    )
```

```python
import functools
import math

import jax
import jax.numpy as jnp
from jax import lax
from jax.experimental import pallas as pl
from jax.experimental.pallas import tpu as pltpu
from jax.sharding import PartitionSpec as P

HEAD = 128
LINK = jnp.bfloat16


def factors_of(count):
    parts = []
    for size in (2, 2, 4):
        size = math.gcd(size, count)
        parts.append(size)
        count //= size
    return parts + [count]


def shift_pairs(count, stride, size, step):
    pairs = []
    for source in range(count):
        part = source // stride % size
        pairs.append((source, source + ((part + step) % size - part) * stride))
    return pairs


def picked(value, index, axis):
    return lax.dynamic_index_in_dim(value, index, axis, keepdims=False)


def total(terms):
    return sum(t.astype(jnp.float32) for t in terms)


def tables(positions):
    freqs = 500000.0 ** (-(jnp.arange(HEAD) % (HEAD // 2)).astype(jnp.float32) / (HEAD // 2))
    angles = positions.astype(jnp.float32)[:, None] * freqs[None, :]
    sign = jnp.where(jnp.arange(HEAD) < HEAD // 2, -1.0, 1.0)
    return jnp.cos(angles), jnp.sin(angles) * sign[None, :]


def after(value, *before):
    return lax.optimization_barrier((value, before))[0]


VMEM = pl.BlockSpec(memory_space=pltpu.VMEM)
PLAIN = pl.BlockSpec(memory_space=pltpu.HBM)


CHEAP = pl.CostEstimate(flops=0, bytes_accessed=0, transcendentals=0)
PARAMS = pltpu.CompilerParams(vmem_limit_bytes=24 * 1024 * 1024)


def turned(block, cosine, sine):
    return block * cosine + pltpu.roll(block, HEAD // 2, 1) * sine


def pack_kernel(
    step, sides, features_ref, documents_ref, sums_ref, out_ref, core_ref, held_ref, wide_ref, half_ref, sems
):
    count, columns = features_ref.shape[0], out_ref.shape[1]
    blocks, fast = sums_ref.shape[:2]
    groups = out_ref.shape[0] // count
    side = lax.rem(lax.axis_index("fsdp") + step, sides)
    core = lax.rem(lax.axis_index("rep") + step, fast)
    ins, outs, wide, half = [], [], [], []
    for i in range(groups):
        at = pl.ds(pl.multiple_of((side * groups + i) * columns, columns), columns)
        rows = pl.ds(i * count, count)
        ins.append(
            pltpu.make_async_copy(features_ref.at[:, at], held_ref.at[rows, :], sems.at[0, i])
        )
        outs.append(pltpu.make_async_copy(held_ref.at[rows, :], out_ref.at[rows, :], sems.at[1, i]))
    for i in range(blocks):
        wide.append(pltpu.make_async_copy(sums_ref.at[i, core], wide_ref.at[i], sems.at[2, i]))
        half.append(pltpu.make_async_copy(half_ref.at[i], core_ref.at[i], sems.at[3, i]))
    for copy in wide + ins:
        copy.start()
    rows = pl.ds(groups * count, out_ref.shape[0] - groups * count)
    held_ref[rows, :] = jnp.zeros((rows.size, columns), out_ref.dtype)
    held_ref[rows, pl.ds(0, count)] = jnp.broadcast_to(
        documents_ref[...].astype(jnp.float32).astype(out_ref.dtype), (rows.size, count)
    )
    outs.append(pltpu.make_async_copy(held_ref.at[rows, :], out_ref.at[rows, :], sems.at[1, groups]))
    outs[-1].start()

    def move_bands():
        for i in range(blocks):
            wide[i].wait()
            half_ref[i] = wide_ref[i].astype(half_ref.dtype)
            half[i].start()

    def move_tokens():
        for i in range(groups):
            ins[i].wait()
            outs[i].start()

    move_bands()
    move_tokens()
    for copy in half + outs:
        copy.wait()


def pack(step, sides, features, documents, sums, note=16):
    blocks, _, band, columns = sums.shape
    count, width = features.shape
    groups = width // sides // columns
    shape = (groups * count + note, columns)
    plain = pl.BlockSpec(memory_space=pltpu.HBM)
    return pl.pallas_call(
        functools.partial(pack_kernel, step, sides),
        in_specs=[plain, VMEM, plain],
        out_specs=[plain, plain],
        out_shape=[
            jax.ShapeDtypeStruct(shape, features.dtype),
            jax.ShapeDtypeStruct((blocks, band, columns), LINK),
        ],
        scratch_shapes=[
            pltpu.VMEM(shape, features.dtype),
            pltpu.VMEM((blocks, band, columns), sums.dtype),
            pltpu.VMEM((blocks, band, columns), LINK),
            pltpu.SemaphoreType.DMA((4, max(groups + 1, blocks))),
        ],
        compiler_params=pltpu.CompilerParams(vmem_limit_bytes=60 * 1024 * 1024),
        cost_estimate=CHEAP,
        name="pack",
    )(features, documents, sums)


def turn_into(out_ref, start, value, cosine, sine):
    for head in range(value.shape[1] // HEAD):
        block = value[:, head * HEAD : (head + 1) * HEAD].astype(jnp.float32)
        block = turned(block, cosine, -sine).astype(out_ref.dtype)
        out_ref[pl.ds(start, value.shape[0]), pl.ds(head * HEAD, HEAD)] = block


def gradient_kernel(side_ref, own_ref, value_ref, cosine_ref, sine_ref, *refs):
    out_ref, rotated_ref = refs[-2:]
    others = [refs[i : i + 4] for i in range(0, len(refs) - 2, 4)]
    count, columns = value_ref.shape

    @pl.when(pl.program_id(0) == 0)
    def _():
        turn_into(rotated_ref, 0, value_ref[...], cosine_ref[...], sine_ref[...])
        for i, (_, value, cosine, sine) in enumerate(others):
            turn_into(rotated_ref, (i + 1) * count, value[...], cosine[...], sine[...])

    tiles = [own_ref[...]] + [ref[...] for other in others for ref in other[:1]]
    out_ref[...] = lax.dot_general(
        jnp.concatenate(tiles, axis=0),
        rotated_ref[...],
        (((0,), (0,)), ((), ())),
        preferred_element_type=jnp.float32,
    ).astype(out_ref.dtype)


def gradient(side, features, value, tables_, others, depth, tile=256):
    count, columns = value.shape
    tiles, wide = depth // tile, columns // tile
    table = pl.BlockSpec((count, HEAD), lambda i, side: (0, 0))
    specs, operands = [], []
    for other in others:
        specs += [
            pl.BlockSpec((count, tile), lambda i, side: (i // wide, i % wide)),
            pl.BlockSpec((count, columns), lambda i, side: (0, 0)),
            table,
            table,
        ]
        operands += other
    return pl.pallas_call(
        gradient_kernel,
        grid_spec=pltpu.PrefetchScalarGridSpec(
            num_scalar_prefetch=1,
            grid=(tiles,),
            in_specs=[
                pl.BlockSpec((count, tile), lambda i, side: (0, side[0] * tiles + i)),
                pl.BlockSpec((count, columns), lambda i, side: (0, 0)),
                table,
                table,
            ]
            + specs,
            out_specs=pl.BlockSpec((tile, columns), lambda i, side: (i, 0)),
            scratch_shapes=[pltpu.VMEM(((len(others) + 1) * count, columns), jnp.bfloat16)],
        ),
        out_shape=jax.ShapeDtypeStruct((depth, columns), jnp.bfloat16),
        compiler_params=PARAMS,
        cost_estimate=CHEAP,
        name="gradient",
    )(side, features, value, *tables_, *operands)


def rotated_into(out_ref, product, cosine_ref, sine_ref):
    cosine, sine = cosine_ref[...], sine_ref[...]
    for head in range(product.shape[1] // HEAD):
        block = product[:, head * HEAD : (head + 1) * HEAD]
        out_ref[:, pl.ds(head * HEAD, HEAD)] = turned(block, cosine, sine).astype(out_ref.dtype)


def product_kernel(side_ref, part_ref, weights_ref, cosine_ref, sine_ref, out_ref, sum_ref):
    at = pl.program_id(0)
    tile = jnp.dot(part_ref[...], weights_ref[...], preferred_element_type=jnp.float32)

    @pl.when(at == 0)
    def _():
        sum_ref[...] = tile

    @pl.when(at > 0)
    def _():
        sum_ref[...] += tile

    @pl.when(at == pl.num_programs(0) - 1)
    def _():
        rotated_into(out_ref, sum_ref[...], cosine_ref, sine_ref)


def product(side, part, weights, cosine, sine, kind, tile=512):
    depth, columns = weights.shape
    tiles, count = depth // tile, cosine.shape[0]
    table = pl.BlockSpec((count, HEAD), lambda i, side: (0, 0))
    return pl.pallas_call(
        product_kernel,
        grid_spec=pltpu.PrefetchScalarGridSpec(
            num_scalar_prefetch=1,
            grid=(tiles,),
            in_specs=[
                pl.BlockSpec((count, tile), lambda i, side: (0, side[0] * tiles + i)),
                pl.BlockSpec((tile, columns), lambda i, side: (i, 0)),
                table,
                table,
            ],
            out_specs=pl.BlockSpec((count, columns), lambda i, side: (0, 0)),
            scratch_shapes=[pltpu.VMEM((count, columns), jnp.float32)],
        ),
        out_shape=jax.ShapeDtypeStruct((count, columns), kind),
        compiler_params=PARAMS,
        cost_estimate=CHEAP,
        name="product",
    )(side, part, weights, cosine, sine)


def project_kernel(count, place_ref, part_ref, cosine_ref, sine_ref, *refs):
    bands, (out_ref, weights_ref, held_ref, sems, part_sems) = refs[:count], refs[count:]
    copies = []
    for ref in bands:
        for i in range(ref.shape[0]):
            rows, at = ref.shape[1], len(copies)
            start = pl.multiple_of(place_ref[at] * rows, rows)
            to = weights_ref.at[pl.ds(start, rows), :]
            copies.append(pltpu.make_async_copy(ref.at[i], to, sems.at[at]))
            copies[-1].start()
    tiles = part_sems.shape[0]
    count, tile = out_ref.shape
    parts = []
    for i in range(tiles):
        rows = pl.ds(i * count, count)
        parts.append(
            pltpu.make_async_copy(part_ref.at[rows, :], held_ref.at[rows, :], part_sems.at[i])
        )
        parts[-1].start()
    for copy in copies:
        copy.wait()
    product = jnp.zeros(out_ref.shape, jnp.float32)
    for i in range(tiles):
        parts[i].wait()
        product += jnp.dot(
            held_ref[pl.ds(i * count, count), :],
            weights_ref[pl.ds(i * tile, tile), :],
            preferred_element_type=jnp.float32,
        )
    rotated_into(out_ref, product, cosine_ref, sine_ref)


def project(places, part, cosine, sine, bands):
    rows = sum(b.shape[0] * b.shape[1] for b in bands)
    count, columns = cosine.shape[0], bands[0].shape[2]
    tiles = rows // columns
    return pl.pallas_call(
        functools.partial(project_kernel, len(bands)),
        in_specs=[pl.BlockSpec(memory_space=pltpu.SMEM), PLAIN, VMEM, VMEM] + [PLAIN] * len(bands),
        out_specs=[VMEM, VMEM],
        out_shape=[
            jax.ShapeDtypeStruct((count, columns), LINK),
            jax.ShapeDtypeStruct((rows, columns), LINK),
        ],
        scratch_shapes=[
            pltpu.VMEM((tiles * count, columns), part.dtype),
            pltpu.SemaphoreType.DMA((places.shape[0],)),
            pltpu.SemaphoreType.DMA((tiles,)),
        ],
        compiler_params=PARAMS,
        cost_estimate=CHEAP,
        name="project",
    )(places, part, cosine, sine, *bands)


def local(tokens, cotangent, doc_ids, pseudo_grads, master, momentum):
    reps = lax.axis_size("rep")
    pair = lax.axis_size("fsdp")
    rep = lax.axis_index("rep")
    side = lax.axis_index("fsdp")
    parts = factors_of(reps)
    strides = [math.prod(parts[:i]) for i in range(len(parts))]
    place = [rep // stride % size for stride, size in zip(strides, parts)]
    band, columns = master.shape[1:]
    features = tokens[0]
    count, width = features.shape
    depth = width // pair

    def moved(value, level, step):
        pairs = shift_pairs(reps, strides[level], parts[level], step)
        return lax.ppermute(value, "rep", pairs)

    def across(value, step):
        return lax.ppermute(value, "fsdp", shift_pairs(pair, 1, pair, step))

    def half_of(step):
        return lax.dynamic_slice_in_dim(features, (side + step) % pair * depth, depth, 1)

    fast, middle, slow, rest = parts
    mine = pseudo_grads[0].reshape(rest, slow, middle, fast, band, columns)
    order = sorted(range(slow), key=lambda k: -min(k, slow - k))

    documents = doc_ids[0]
    which = side.astype(jnp.int32).reshape(1)
    bands = pseudo_grads[0].reshape(-1, fast, band, columns)
    sent, out = [], []
    for step in range(1, max(pair, fast)):
        one, two = pack(step, pair, features, doc_ids, bands)
        sent += [one] if step < pair else []
        out += [two.reshape(rest, slow, middle, band, columns)] if step < fast else []
    parted = [None] + [across(t, i + 1) for i, t in enumerate(sent)][::-1]

    cores = [moved(t, 0, i + 1) for i, t in enumerate(out)]

    def piece(k, step):
        terms = [picked(mine, place[0], 3)] + cores
        terms = [picked(t, (place[2] + k) % slow, 1) for t in terms]
        return [picked(t, (place[1] + step) % middle, 1) for t in terms]

    out = {k: [total(piece(k, i)).astype(LINK) for i in range(1, middle)] for k in order}
    sums = {k: [moved(t, 1, i + 1) for i, t in enumerate(out[k])] for k in order}
    last = out
    received = []
    for k in order:
        if k:
            out = total(piece(k, 0) + after(sums[k], last)).astype(LINK)
            last = out
            received.append(moved(out, 2, k))
        else:
            received = piece(k, 0) + sums[k] + received
    here = [picked(t, place[3], 0) for t in received]
    for step in range(1, rest):
        chosen = total([picked(t, (place[3] + step) % rest, 0) for t in received])
        here.append(moved(chosen.astype(LINK), 3, step))
    upstream = after(cotangent[0], last)
    upstream = [None] + [across(upstream, pair - step) for step in range(1, pair)]

    def updated(delta):
        new_momentum = 0.9 * momentum[0] + delta
        return master[0] - 0.7 * (delta + 0.9 * new_momentum), new_momentum

    outer_delta = total(here) / reps

    held = updated(outer_delta)[0].astype(LINK)[None]
    held = jnp.concatenate([held] + [moved(held, 3, rest - k) for k in range(1, rest)])
    outer = [(place[3] + k) % rest * strides[3] for k in range(rest)]
    order = sorted(range(slow), key=lambda k: min(k, slow - k))
    slows = {k: held if k == 0 else moved(held, 2, slow - k) for k in order}
    crossed = {
        (k, shift): moved(slows[k], 1, middle - shift) for shift in range(1, middle) for k in order
    }
    near = [key for key in crossed if key[0] != order[-1]]
    last = [key for key in crossed if key[0] == order[-1]]
    groups = [[(k, 0) for k in order], near + last]
    crossed.update({(k, 0): slows[k] for k in order})
    bands, places = [], []
    for keys in groups:
        if not keys:
            continue
        group = [crossed[key] for key in keys]
        base = [
            o + (place[2] + k) % slow * strides[2] + (place[1] + shift) % middle * strides[1]
            for k, shift in keys
            for o in outer
        ]
        joined = group[0] if len(group) == 1 else jnp.concatenate(group)
        bands += group
        places += [spot + place[0] for spot in base]
        for step in range(1, fast):
            bands.append(moved(joined, 0, fast - step))
            places += [spot + (place[0] + step) % fast for spot in base]
    places = jnp.stack(places)

    early = [documents] + [
        part[depth // columns * count, :count].astype(jnp.int32) for part in parted[1:]
    ]
    turns = []
    for step, docs in enumerate(early):
        at = (side + step) % pair * count + jnp.arange(count, dtype=jnp.int32)
        for others in early:
            at = at - jnp.sum((others[None, :] < docs[:, None]).astype(jnp.int32), axis=1)
        turns.append(tables(at))

    other = []
    for step in range(1, pair):
        out, weights = project(places, parted[step], *turns[step], bands)
        other.append(across(out, pair - step))
    features = after(features, weights)
    grads = gradient(
        which,
        features,
        cotangent[0],
        turns[0],
        [(parted[step], upstream[step], *turns[step]) for step in range(1, pair)],
        depth,
    )
    keys = total([product(which, features, weights, *turns[0], jnp.float32)] + other)
    keys = keys.astype(jnp.bfloat16)
    new_master, new_momentum = updated(after(outer_delta, weights))
    return (
        new_master[None],
        new_momentum[None],
        keys[None],
        grads[None],
    )


def solution(mesh):
    return jax.shard_map(
        local,
        mesh=mesh,
        in_specs=(
            P("rep", "fsdp", None),
            P("rep", "fsdp", None),
            P("rep", "fsdp"),
            P("rep", "fsdp", None),
            P("fsdp", "rep", None),
            P("fsdp", "rep", None),
        ),
        out_specs=(
            P("fsdp", "rep", None),
            P("fsdp", "rep", None),
            P("rep", "fsdp", None),
            P("rep", "fsdp", None),
        ),
        check_vma=False,
    )
```

```python
import functools
import math

import jax
import jax.numpy as jnp
from jax import lax
from jax.experimental import pallas as pl
from jax.experimental.pallas import tpu as pltpu
from jax.sharding import PartitionSpec as P

HEAD = 128
LINK = jnp.bfloat16
SHARES = 2


def factors_of(count):
    parts = []
    for size in (2, 2, 4):
        size = math.gcd(size, count)
        parts.append(size)
        count //= size
    return parts + [count]


def shift_pairs(count, stride, size, step):
    pairs = []
    for source in range(count):
        part = source // stride % size
        pairs.append((source, source + ((part + step) % size - part) * stride))
    return pairs


def picked(value, index, axis):
    return lax.dynamic_index_in_dim(value, index, axis, keepdims=False)


def total(terms):
    return sum(t.astype(jnp.float32) for t in terms)


def tables(positions):
    freqs = 500000.0 ** (-(jnp.arange(HEAD) % (HEAD // 2)).astype(jnp.float32) / (HEAD // 2))
    angles = positions.astype(jnp.float32)[:, None] * freqs[None, :]
    sign = jnp.where(jnp.arange(HEAD) < HEAD // 2, -1.0, 1.0)
    return jnp.cos(angles), jnp.sin(angles) * sign[None, :]


def after(value, *before):
    return lax.optimization_barrier((value, before))[0]


VMEM = pl.BlockSpec(memory_space=pltpu.VMEM)
PLAIN = pl.BlockSpec(memory_space=pltpu.HBM)


CHEAP = pl.CostEstimate(flops=0, bytes_accessed=0, transcendentals=0)
PARAMS = pltpu.CompilerParams(vmem_limit_bytes=24 * 1024 * 1024)


def turned(block, cosine, sine):
    return block * cosine + pltpu.roll(block, HEAD // 2, 1) * sine


def pack_kernel(
    step, sides, features_ref, documents_ref, sums_ref, out_ref, core_ref, held_ref, wide_ref, half_ref, sems
):
    count, columns = features_ref.shape[0], out_ref.shape[1]
    blocks, fast = sums_ref.shape[:2]
    groups = out_ref.shape[0] // count
    side = lax.rem(lax.axis_index("fsdp") + step, sides)
    core = lax.rem(lax.axis_index("rep") + step, fast)
    ins, outs, wide, half = [], [], [], []
    for i in range(groups):
        at = pl.ds(pl.multiple_of((side * groups + i) * columns, columns), columns)
        rows = pl.ds(i * count, count)
        ins.append(
            pltpu.make_async_copy(features_ref.at[:, at], held_ref.at[rows, :], sems.at[0, i])
        )
        outs.append(pltpu.make_async_copy(held_ref.at[rows, :], out_ref.at[rows, :], sems.at[1, i]))
    chunks = [pl.ds(i * blocks // SHARES, blocks // SHARES) for i in range(SHARES)]
    for i, at in enumerate(chunks):
        wide.append(pltpu.make_async_copy(sums_ref.at[at, core], wide_ref.at[at], sems.at[2, i]))
        half.append(pltpu.make_async_copy(half_ref.at[at], core_ref.at[at], sems.at[3, i]))
    for copy in wide + ins:
        copy.start()
    rows = pl.ds(groups * count, out_ref.shape[0] - groups * count)
    held_ref[rows, :] = jnp.zeros((rows.size, columns), out_ref.dtype)
    held_ref[rows, pl.ds(0, count)] = jnp.broadcast_to(
        documents_ref[...].astype(jnp.float32).astype(out_ref.dtype), (rows.size, count)
    )
    outs.append(pltpu.make_async_copy(held_ref.at[rows, :], out_ref.at[rows, :], sems.at[1, groups]))
    outs[-1].start()

    def move_bands():
        for i, at in enumerate(chunks):
            wide[i].wait()
            half_ref[at] = wide_ref[at].astype(half_ref.dtype)
            half[i].start()

    def move_tokens():
        for i in range(groups):
            ins[i].wait()
            outs[i].start()

    move_bands()
    move_tokens()
    for copy in half + outs:
        copy.wait()


def pack(step, sides, features, documents, sums, note=16):
    blocks, _, band, columns = sums.shape
    count, width = features.shape
    groups = width // sides // columns
    shape = (groups * count + note, columns)
    plain = pl.BlockSpec(memory_space=pltpu.HBM)
    return pl.pallas_call(
        functools.partial(pack_kernel, step, sides),
        in_specs=[plain, VMEM, plain],
        out_specs=[plain, plain],
        out_shape=[
            jax.ShapeDtypeStruct(shape, features.dtype),
            jax.ShapeDtypeStruct((blocks, band, columns), LINK),
        ],
        scratch_shapes=[
            pltpu.VMEM(shape, features.dtype),
            pltpu.VMEM((blocks, band, columns), sums.dtype),
            pltpu.VMEM((blocks, band, columns), LINK),
            pltpu.SemaphoreType.DMA((4, max(groups + 1, SHARES))),
        ],
        compiler_params=pltpu.CompilerParams(vmem_limit_bytes=60 * 1024 * 1024),
        cost_estimate=CHEAP,
        name="pack",
    )(features, documents, sums)


def turn_into(out_ref, start, value, cosine, sine):
    for head in range(value.shape[1] // HEAD):
        block = value[:, head * HEAD : (head + 1) * HEAD].astype(jnp.float32)
        block = turned(block, cosine, -sine).astype(out_ref.dtype)
        out_ref[pl.ds(start, value.shape[0]), pl.ds(head * HEAD, HEAD)] = block


def gradient_kernel(side_ref, own_ref, value_ref, cosine_ref, sine_ref, *refs):
    out_ref, rotated_ref = refs[-2:]
    others = [refs[i : i + 4] for i in range(0, len(refs) - 2, 4)]
    count, columns = value_ref.shape

    @pl.when(pl.program_id(0) == 0)
    def _():
        turn_into(rotated_ref, 0, value_ref[...], cosine_ref[...], sine_ref[...])
        for i, (_, value, cosine, sine) in enumerate(others):
            turn_into(rotated_ref, (i + 1) * count, value[...], cosine[...], sine[...])

    tiles = [own_ref[...]] + [ref[...] for other in others for ref in other[:1]]
    out_ref[...] = lax.dot_general(
        jnp.concatenate(tiles, axis=0),
        rotated_ref[...],
        (((0,), (0,)), ((), ())),
        preferred_element_type=jnp.float32,
    ).astype(out_ref.dtype)


def gradient(side, features, value, tables_, others, depth, tile=256):
    count, columns = value.shape
    tiles, wide = depth // tile, columns // tile
    table = pl.BlockSpec((count, HEAD), lambda i, side: (0, 0))
    specs, operands = [], []
    for other in others:
        specs += [
            pl.BlockSpec((count, tile), lambda i, side: (i // wide, i % wide)),
            pl.BlockSpec((count, columns), lambda i, side: (0, 0)),
            table,
            table,
        ]
        operands += other
    return pl.pallas_call(
        gradient_kernel,
        grid_spec=pltpu.PrefetchScalarGridSpec(
            num_scalar_prefetch=1,
            grid=(tiles,),
            in_specs=[
                pl.BlockSpec((count, tile), lambda i, side: (0, side[0] * tiles + i)),
                pl.BlockSpec((count, columns), lambda i, side: (0, 0)),
                table,
                table,
            ]
            + specs,
            out_specs=pl.BlockSpec((tile, columns), lambda i, side: (i, 0)),
            scratch_shapes=[pltpu.VMEM(((len(others) + 1) * count, columns), jnp.bfloat16)],
        ),
        out_shape=jax.ShapeDtypeStruct((depth, columns), jnp.bfloat16),
        compiler_params=PARAMS,
        cost_estimate=CHEAP,
        name="gradient",
    )(side, features, value, *tables_, *operands)


def rotated_into(out_ref, product, cosine_ref, sine_ref):
    cosine, sine = cosine_ref[...], sine_ref[...]
    for head in range(product.shape[1] // HEAD):
        block = product[:, head * HEAD : (head + 1) * HEAD]
        out_ref[:, pl.ds(head * HEAD, HEAD)] = turned(block, cosine, sine).astype(out_ref.dtype)


def product_kernel(side_ref, part_ref, weights_ref, cosine_ref, sine_ref, out_ref, sum_ref):
    at = pl.program_id(0)
    tile = jnp.dot(part_ref[...], weights_ref[...], preferred_element_type=jnp.float32)

    @pl.when(at == 0)
    def _():
        sum_ref[...] = tile

    @pl.when(at > 0)
    def _():
        sum_ref[...] += tile

    @pl.when(at == pl.num_programs(0) - 1)
    def _():
        rotated_into(out_ref, sum_ref[...], cosine_ref, sine_ref)


def product(side, part, weights, cosine, sine, kind, tile=512):
    depth, columns = weights.shape
    tiles, count = depth // tile, cosine.shape[0]
    table = pl.BlockSpec((count, HEAD), lambda i, side: (0, 0))
    return pl.pallas_call(
        product_kernel,
        grid_spec=pltpu.PrefetchScalarGridSpec(
            num_scalar_prefetch=1,
            grid=(tiles,),
            in_specs=[
                pl.BlockSpec((count, tile), lambda i, side: (0, side[0] * tiles + i)),
                pl.BlockSpec((tile, columns), lambda i, side: (i, 0)),
                table,
                table,
            ],
            out_specs=pl.BlockSpec((count, columns), lambda i, side: (0, 0)),
            scratch_shapes=[pltpu.VMEM((count, columns), jnp.float32)],
        ),
        out_shape=jax.ShapeDtypeStruct((count, columns), kind),
        compiler_params=PARAMS,
        cost_estimate=CHEAP,
        name="product",
    )(side, part, weights, cosine, sine)


def project_kernel(count, place_ref, part_ref, cosine_ref, sine_ref, *refs):
    bands, (out_ref, weights_ref, held_ref, sems, part_sems) = refs[:count], refs[count:]
    copies = []
    for ref in bands:
        for i in range(ref.shape[0]):
            rows, at = ref.shape[1], len(copies)
            start = pl.multiple_of(place_ref[at] * rows, rows)
            to = weights_ref.at[pl.ds(start, rows), :]
            copies.append(pltpu.make_async_copy(ref.at[i], to, sems.at[at]))
            copies[-1].start()
    tiles = part_sems.shape[0]
    count, tile = out_ref.shape
    parts = []
    for i in range(tiles):
        rows = pl.ds(i * count, count)
        parts.append(
            pltpu.make_async_copy(part_ref.at[rows, :], held_ref.at[rows, :], part_sems.at[i])
        )
        parts[-1].start()
    for copy in copies:
        copy.wait()
    product = jnp.zeros(out_ref.shape, jnp.float32)
    for i in range(tiles):
        parts[i].wait()
        product += jnp.dot(
            held_ref[pl.ds(i * count, count), :],
            weights_ref[pl.ds(i * tile, tile), :],
            preferred_element_type=jnp.float32,
        )
    rotated_into(out_ref, product, cosine_ref, sine_ref)


def project(places, part, cosine, sine, bands):
    rows = sum(b.shape[0] * b.shape[1] for b in bands)
    count, columns = cosine.shape[0], bands[0].shape[2]
    tiles = rows // columns
    return pl.pallas_call(
        functools.partial(project_kernel, len(bands)),
        in_specs=[pl.BlockSpec(memory_space=pltpu.SMEM), PLAIN, VMEM, VMEM] + [PLAIN] * len(bands),
        out_specs=[VMEM, VMEM],
        out_shape=[
            jax.ShapeDtypeStruct((count, columns), LINK),
            jax.ShapeDtypeStruct((rows, columns), LINK),
        ],
        scratch_shapes=[
            pltpu.VMEM((tiles * count, columns), part.dtype),
            pltpu.SemaphoreType.DMA((places.shape[0],)),
            pltpu.SemaphoreType.DMA((tiles,)),
        ],
        compiler_params=PARAMS,
        cost_estimate=CHEAP,
        name="project",
    )(places, part, cosine, sine, *bands)


def local(tokens, cotangent, doc_ids, pseudo_grads, master, momentum):
    reps = lax.axis_size("rep")
    pair = lax.axis_size("fsdp")
    rep = lax.axis_index("rep")
    side = lax.axis_index("fsdp")
    parts = factors_of(reps)
    strides = [math.prod(parts[:i]) for i in range(len(parts))]
    place = [rep // stride % size for stride, size in zip(strides, parts)]
    band, columns = master.shape[1:]
    features = tokens[0]
    count, width = features.shape
    depth = width // pair

    def moved(value, level, step):
        pairs = shift_pairs(reps, strides[level], parts[level], step)
        return lax.ppermute(value, "rep", pairs)

    def across(value, step):
        return lax.ppermute(value, "fsdp", shift_pairs(pair, 1, pair, step))

    def half_of(step):
        return lax.dynamic_slice_in_dim(features, (side + step) % pair * depth, depth, 1)

    fast, middle, slow, rest = parts
    mine = pseudo_grads[0].reshape(rest, slow, middle, fast, band, columns)
    order = sorted(range(slow), key=lambda k: -min(k, slow - k))

    documents = doc_ids[0]
    which = side.astype(jnp.int32).reshape(1)
    bands = pseudo_grads[0].reshape(-1, fast, band, columns)
    sent, out = [], []
    for step in range(1, max(pair, fast)):
        one, two = pack(step, pair, features, doc_ids, bands)
        sent += [one] if step < pair else []
        out += [two.reshape(rest, slow, middle, band, columns)] if step < fast else []
    parted = [None] + [across(t, i + 1) for i, t in enumerate(sent)][::-1]

    cores = [moved(t, 0, i + 1) for i, t in enumerate(out)]

    def piece(k, step):
        terms = [picked(mine, place[0], 3)] + cores
        terms = [picked(t, (place[2] + k) % slow, 1) for t in terms]
        return [picked(t, (place[1] + step) % middle, 1) for t in terms]

    out = {k: [total(piece(k, i)).astype(LINK) for i in range(1, middle)] for k in order}
    sums = {k: [moved(t, 1, i + 1) for i, t in enumerate(out[k])] for k in order}
    last = out
    received = []
    for k in order:
        if k:
            out = total(piece(k, 0) + after(sums[k], last)).astype(LINK)
            last = out
            received.append(moved(out, 2, k))
        else:
            received = piece(k, 0) + sums[k] + received
    here = [picked(t, place[3], 0) for t in received]
    for step in range(1, rest):
        chosen = total([picked(t, (place[3] + step) % rest, 0) for t in received])
        here.append(moved(chosen.astype(LINK), 3, step))
    upstream = after(cotangent[0], last)
    upstream = [None] + [across(upstream, pair - step) for step in range(1, pair)]

    def updated(delta):
        new_momentum = 0.9 * momentum[0] + delta
        return master[0] - 0.7 * (delta + 0.9 * new_momentum), new_momentum

    outer_delta = total(here) / reps

    held = updated(outer_delta)[0].astype(LINK)[None]
    held = jnp.concatenate([held] + [moved(held, 3, rest - k) for k in range(1, rest)])
    outer = [(place[3] + k) % rest * strides[3] for k in range(rest)]
    order = sorted(range(slow), key=lambda k: min(k, slow - k))
    slows = {k: held if k == 0 else moved(held, 2, slow - k) for k in order}
    crossed = {
        (k, shift): moved(slows[k], 1, middle - shift) for shift in range(1, middle) for k in order
    }
    near = [key for key in crossed if key[0] != order[-1]]
    last = [key for key in crossed if key[0] == order[-1]]
    groups = [[(k, 0) for k in order], near + last]
    crossed.update({(k, 0): slows[k] for k in order})
    bands, places = [], []
    for keys in groups:
        if not keys:
            continue
        group = [crossed[key] for key in keys]
        base = [
            o + (place[2] + k) % slow * strides[2] + (place[1] + shift) % middle * strides[1]
            for k, shift in keys
            for o in outer
        ]
        joined = group[0] if len(group) == 1 else jnp.concatenate(group)
        bands += group
        places += [spot + place[0] for spot in base]
        for step in range(1, fast):
            bands.append(moved(joined, 0, fast - step))
            places += [spot + (place[0] + step) % fast for spot in base]
    places = jnp.stack(places)

    early = [documents] + [
        part[depth // columns * count, :count].astype(jnp.int32) for part in parted[1:]
    ]
    turns = []
    for step, docs in enumerate(early):
        at = (side + step) % pair * count + jnp.arange(count, dtype=jnp.int32)
        for others in early:
            at = at - jnp.sum((others[None, :] < docs[:, None]).astype(jnp.int32), axis=1)
        turns.append(tables(at))

    other = []
    for step in range(1, pair):
        out, weights = project(places, parted[step], *turns[step], bands)
        other.append(across(out, pair - step))
    features = after(features, weights)
    grads = gradient(
        which,
        features,
        cotangent[0],
        turns[0],
        [(parted[step], upstream[step], *turns[step]) for step in range(1, pair)],
        depth,
    )
    keys = total([product(which, features, weights, *turns[0], jnp.float32)] + other)
    keys = keys.astype(jnp.bfloat16)
    new_master, new_momentum = updated(after(outer_delta, weights))
    return (
        new_master[None],
        new_momentum[None],
        keys[None],
        grads[None],
    )


def solution(mesh):
    return jax.shard_map(
        local,
        mesh=mesh,
        in_specs=(
            P("rep", "fsdp", None),
            P("rep", "fsdp", None),
            P("rep", "fsdp"),
            P("rep", "fsdp", None),
            P("fsdp", "rep", None),
            P("fsdp", "rep", None),
        ),
        out_specs=(
            P("fsdp", "rep", None),
            P("fsdp", "rep", None),
            P("rep", "fsdp", None),
            P("rep", "fsdp", None),
        ),
        check_vma=False,
    )
```
